256 devices in a mesh: pair: 64 (over x, y, z_lo), orb: 4 (over z_hi, core).
Axes of the slice: x: 4, y: 4, z: 8 (z_hi: 2, z_lo: 4; z = z_hi * 4 + z_lo), core: 2. Of those that a mesh axis runs over, the one named last changes fastest.
Arguments:
- ao_slab: bfloat16 [512, 1224, 1224], P('pair', 'orb'), may hold values from -9 to 9, as said below
- occ_coef: bfloat16 [1224, 200], replicated, may hold values from -0.15625 to 0.15625
- vir_coef: bfloat16 [1224, 1024], P(None, 'orb'), may hold values from -1.5 to 1.5
- tile_index: int32 [16], replicated, may hold values from 0 to 1223
- pair_order: int32 [20160], replicated, may hold values from 0 to 20159, each once
Outputs:
- mixed_block: bfloat16 [20160, 32, 1024], P('pair', None, 'orb')
The draws below stay inside these ranges and needn't reach their ends.
Inputs may be any that keep to these rules, and one draw needn't show every extreme that they name: ao_slab[rs, p, q] equals ao_slab[rs, q, p].
All inputs are finite; a program needn't handle non-finite values.
Results may differ from the reference program's by a relative error of at most 0.0057.
Values may be sent and summed in bfloat16 or wider, within the bound.
No kernel may reach another device: no remote copies, remote signals or barrier semaphores. Data moves between devices by JAX's collectives and lax.ppermute only.
A program may use at most 128 MiB of HBM per device.

```python
import math
import jax
import jax.numpy as jnp
import numpy as np
from jax import lax

NAO = 1224
NOCC = 200
NVIR = 1024
TS = 16
RS = 512
TR = 32
NPAIRS = 20100
NPAD = 20160
PAIR_DEV = 315
N_PAIR = 64


def draw_ao_slab(key, part):
    key = jax.random.fold_in(key, 1)
    base = jnp.clip(jax.random.normal(key, (RS, NAO, NAO), jnp.float32), -6.0, 6.0)
    sym = (base + jnp.swapaxes(base, 1, 2)) * math.sqrt(0.5)
    return sym.astype(jnp.bfloat16)


def touch_ends(entries, key, low, top_value):
    dims = entries.shape
    index_at = [jax.random.randint(jax.random.fold_in(key, axis), (), 0, dims[axis]) for axis in range(len(dims))]
    entries = entries.at[tuple(index_at)].set(low)
    longest = dims.index(max(dims))
    index_at[longest] = (index_at[longest] + 1) % dims[longest]
    return entries.at[tuple(index_at)].set(top_value)


def level_of(own_key, extent, split, least, top_value):
    gain = 1.0
    for dim, parts in split:
        draws = jax.random.uniform(jax.random.fold_in(jax.random.fold_in(own_key, 6), dim), (parts,), jnp.float32, least / len(split), top_value / len(split))
        gain = gain * jnp.repeat(jnp.exp(draws), extent[dim] // parts).reshape((-1,) + (1,) * (len(extent) - 1 - dim))
    return gain


def normal_values(stream_key, extent, scale, reach, cuts=(), held_as=jnp.bfloat16):
    gain = level_of(stream_key, extent, cuts, -0.22, 0.18) if cuts else 1.0
    array = jax.random.normal(stream_key, extent, jnp.float32) * scale * gain
    return jnp.minimum(jnp.maximum(array, -reach), reach).astype(held_as)


def setup_inputs(seed: int = 0) -> dict:
    key_of = jax.random.split(jax.random.key(seed), 6)
    return {
        "ao_slab": draw_ao_slab(jax.random.fold_in(key_of[5], 71), 0),
        "occ_coef": normal_values(key_of[1], (NAO, NOCC), NAO ** -0.5, 0.15625),
        "vir_coef": normal_values(key_of[2], (NAO, NVIR), TS ** -0.5, 1.5, ((1, 4),)),
        "tile_index": touch_ends(jax.random.randint(key_of[3], (TS,), 0, NAO), jax.random.fold_in(key_of[3], 1), 0, NAO - 1).astype(jnp.int32),
        "pair_order": jax.random.permutation(key_of[4], NPAD).astype(jnp.int32),
    }


def reference(ao_slab, occ_coef, vir_coef, tile_index, pair_order):
    def quarter(slab):
        first = jnp.dot(slab, occ_coef, preferred_element_type=jnp.float32).astype(jnp.bfloat16)
        half = jnp.dot(occ_coef.T, first, preferred_element_type=jnp.float32).astype(jnp.bfloat16)
        return half.reshape(-1)

    half = lax.map(quarter, ao_slab)
    lower = np.tril_indices(NOCC)
    packed_cols = jnp.asarray((lower[0] * NOCC + lower[1]).astype(np.int32))
    order = pair_order.astype(jnp.int32)
    valid = (order < NPAIRS).astype(jnp.float32)
    columns_all = packed_cols[jnp.minimum(order, NPAIRS - 1)]
    vir_rows = vir_coef[tile_index.astype(jnp.int32)].astype(jnp.float32)
    owner_cols = columns_all.reshape(N_PAIR, PAIR_DEV)
    owner_valid = valid.reshape(N_PAIR, PAIR_DEV)

    def block(packed):
        indices, keep = packed
        columns = half[:, indices].reshape(TR, TS, PAIR_DEV).astype(jnp.float32) * keep
        return jnp.einsum("rsp,sb->prb", columns, vir_rows).astype(jnp.bfloat16)

    result = lax.map(block, (owner_cols, owner_valid))
    return result.reshape(NPAD, TR, NVIR)
```

```python
import jax
import jax.numpy as jnp
from jax import lax
from jax.experimental import pallas as pl
from jax.experimental.pallas import tpu as pltpu
from jax.sharding import PartitionSpec as P

NOCC = 200
COLS = 88
ROWS = 256
NPAIRS = NOCC * (NOCC + 1) // 2
KPER = 4
SLOT = 320
CHUNK = 4 * SLOT


def fold(pair_order):
    t = pair_order
    root = jnp.sqrt(8.0 * t.astype(jnp.float32) + 1.0)
    i = ((root - 1.0) * 0.5).astype(jnp.int32)
    i = jnp.where(i * (i + 1) // 2 > t, i - 1, i)
    i = jnp.where((i + 1) * (i + 2) // 2 <= t, i + 1, i)
    j = t - i * (i + 1) // 2
    row = jnp.where(j < 88, i, jnp.where(j >= 113, j - 113, jnp.where(i >= 112, j + 112, j + 137)))
    col = jnp.where(j < 88, j, jnp.where((j >= 113) | (i >= 112), i - 112, i - 88))
    return row, jnp.where(t < NPAIRS, col, -1)


def half_kernel(core_ref, ao_ref, ct_ref, ctp_ref, keep_ref, send_ref, first_ref):
    step = pl.program_id(0)
    block, kk, nq = ao_ref.shape
    slab = ao_ref[...].reshape(block * kk, nq)
    first = lax.dot_general(slab, ct_ref[...], (((1,), (1,)), ((), ())), preferred_element_type=jnp.float32)
    at = pl.ds(pl.multiple_of(step * (block * kk), 8), block * kk)
    first_ref[0, at, :] = first[:, 0:128]
    first_ref[1, at, 0:NOCC - 128] = first[:, 128:NOCC]

    @pl.when(step == pl.num_programs(0) - 1)
    def _():
        core = core_ref[0]
        np_ = first_ref.shape[1] // kk
        lane = lax.broadcasted_iota(jnp.int32, (COLS, ROWS), 1)
        col = lax.broadcasted_iota(jnp.int32, (COLS, ROWS), 0)
        ctp = ctp_ref[...]

        def folded(k):
            at = pl.ds(k, np_, stride=kk)
            fk = jnp.concatenate([first_ref[0, at, :], first_ref[1, at, :]], axis=1)
            fk = jnp.where(lax.broadcasted_iota(jnp.int32, fk.shape, 1) < NOCC, fk, 0.0).astype(jnp.bfloat16)
            out = jnp.dot(ctp, fk, preferred_element_type=jnp.float32)
            o1 = out[0:88]
            o2 = out[88:176]
            o3 = jnp.concatenate([out[176:200], jnp.zeros((64, ROWS), jnp.float32)], axis=0)
            tri = jnp.where(lane >= col, o1, pltpu.roll(o2, ROWS - 113, 1))
            rest = jnp.where(lane < 225, pltpu.roll(o2, 112, 1), pltpu.roll(o3, 137, 1))
            return jnp.where(lane < NOCC, tri, jnp.where(lane < 249, rest, 0.0))

        for k in range(KPER):
            send_ref[k] = folded(KPER * (1 - core) + k).astype(jnp.bfloat16)
        for k in range(KPER):
            keep_ref[k] = folded(KPER * core + k)


def select_kernel(row_ref, col_ref, keep_ref, recv_ref, out_ref, tri_ref):
    for k in range(KPER):
        tri_ref[k * COLS:(k + 1) * COLS, :] = (keep_ref[k] + recv_ref[k].astype(jnp.float32)).astype(jnp.bfloat16)

    @pl.loop(0, row_ref.shape[0])
    def _(ch):
        row = row_ref[ch]
        col = col_ref[ch]
        hot = (lax.broadcasted_iota(jnp.int32, (ROWS, CHUNK), 0) == row).astype(jnp.bfloat16)
        picked = jnp.dot(tri_ref[...], hot, preferred_element_type=jnp.float32)
        mask = lax.broadcasted_iota(jnp.int32, (COLS, CHUNK), 0) == col
        vals = [
            jnp.sum(jnp.where(mask, picked[k * COLS:(k + 1) * COLS], 0.0), axis=0, keepdims=True)
            for k in range(KPER)
        ]
        vals = jnp.concatenate(vals, axis=0)
        lane = lax.broadcasted_iota(jnp.int32, (2, 2 * SLOT), 1)
        for u in range(2):
            here = vals[:, 2 * SLOT * u:2 * SLOT * (u + 1)]
            moved = pltpu.roll(here, SLOT, 1)
            even = jnp.where(lane < SLOT, here[0:2], moved[2:4]).astype(jnp.bfloat16)
            odd = jnp.where(lane < SLOT, moved[0:2], here[2:4]).astype(jnp.bfloat16)
            at = ch * 8 + u * 4
            out_ref[at] = even
            out_ref[at + 1] = even
            out_ref[at + 2] = odd
            out_ref[at + 3] = odd


def final_kernel(core_ref, own_ref, other_ref, vir_ref, out_ref, turned_ref, vbig_ref):
    step = pl.program_id(0)
    block = out_ref.shape[0]

    @pl.when(step == 0)
    def _():
        core = core_ref[0]
        line = lax.broadcasted_iota(jnp.int32, (256, 16), 0)
        s = lax.broadcasted_iota(jnp.int32, (256, 16), 1)
        src_core = jnp.where(line < 128, core, 1 - core)
        want = ((line % 8) // 4) * 8 + 4 * src_core + line % 2 + 2 * ((line % 128) // 64)
        hot = (s == want).astype(jnp.bfloat16)
        vbig_ref[...] = jnp.dot(hot, vir_ref[...], preferred_element_type=jnp.float32).astype(jnp.bfloat16)
        for g in range(4):
            for n, ref in enumerate((own_ref, other_ref)):
                part = ref[32 * g:32 * (g + 1)].astype(jnp.float32).reshape(64, 2 * SLOT)
                wide = jnp.concatenate([part[:, 0:SLOT], part[:, SLOT:2 * SLOT]], axis=0)
                turned_ref[g, :, 128 * n:128 * (n + 1)] = wide.T

    lane = lax.broadcasted_iota(jnp.int32, (8, 256), 1)
    mask = (lane % 64) // 8 == lax.broadcasted_iota(jnp.int32, (8, 256), 0)
    at = pl.multiple_of(step * block, 8)
    for pair in range(2):
        parts = []
        for g in (2 * pair, 2 * pair + 1):
            rows = turned_ref[g, pl.ds(at, block), :]
            parts.append(jnp.where(mask[None], jnp.broadcast_to(rows[:, None, :], (block, 8, 256)), 0.0))
        lhs = jnp.concatenate(parts, axis=1).reshape(block * 16, 256).astype(jnp.bfloat16)
        res = jnp.dot(lhs, vbig_ref[...], preferred_element_type=jnp.float32)
        out_ref[:, 16 * pair:16 * (pair + 1), :] = res.reshape(block, 16, 256).astype(jnp.bfloat16)


def half_stage(core, slab, ct, ctp):
    np_, kk, nq = slab.shape
    block = 51
    kept = pl.BlockSpec((KPER, COLS, ROWS), lambda i: (0, 0, 0))
    return pl.pallas_call(
        half_kernel,
        grid=(np_ // block,),
        in_specs=[
            pl.BlockSpec(memory_space=pltpu.SMEM),
            pl.BlockSpec((block, kk, nq), lambda i: (i, 0, 0)),
            pl.BlockSpec((NOCC, nq), lambda i: (0, 0)),
            pl.BlockSpec((NOCC, np_), lambda i: (0, 0)),
        ],
        out_specs=[kept, kept],
        out_shape=[
            jax.ShapeDtypeStruct((KPER, COLS, ROWS), jnp.float32),
            jax.ShapeDtypeStruct((KPER, COLS, ROWS), jnp.bfloat16),
        ],
        scratch_shapes=[pltpu.VMEM((2, np_ * kk, 128), jnp.float32)],
        compiler_params=pltpu.CompilerParams(vmem_limit_bytes=48 * 2**20),
        name="half",
    )(core, slab, ct, ctp)


def places_of(pair_order, n_pair):
    owned = pair_order.shape[0] // n_pair
    row, col = fold(pair_order)
    pads = ((0, 0), (0, SLOT - owned))
    row = jnp.pad(row.reshape(n_pair, owned), pads).reshape(-1, 1, CHUNK)
    col = jnp.pad(col.reshape(n_pair, owned), pads, constant_values=-1).reshape(-1, 1, CHUNK)
    return row, col


def select_stage(row, col, keep, recv):
    n_dest = 2 * row.shape[0] * CHUNK // SLOT
    return pl.pallas_call(
        select_kernel,
        out_shape=jax.ShapeDtypeStruct((n_dest, 2, 2 * SLOT), jnp.bfloat16),
        in_specs=[pl.BlockSpec(memory_space=pltpu.VMEM)] * 4,
        out_specs=pl.BlockSpec(memory_space=pltpu.VMEM),
        scratch_shapes=[pltpu.VMEM((KPER * COLS, ROWS), jnp.bfloat16)],
        compiler_params=pltpu.CompilerParams(vmem_limit_bytes=48 * 2**20),
        name="select",
    )(row, col, keep, recv)


def final_stage(core, own, other, vir_rows, owned):
    block = 40
    full = pl.BlockSpec(own.shape, lambda i: (0, 0, 0))
    return pl.pallas_call(
        final_kernel,
        grid=(pl.cdiv(owned, block),),
        in_specs=[
            pl.BlockSpec(memory_space=pltpu.SMEM),
            full,
            full,
            pl.BlockSpec((16, 256), lambda i: (0, 0)),
        ],
        out_specs=pl.BlockSpec((block, 32, 256), lambda i: (i, 0, 0)),
        out_shape=jax.ShapeDtypeStruct((owned, 32, 256), jnp.bfloat16),
        scratch_shapes=[pltpu.VMEM((4, SLOT, 256), jnp.float32), pltpu.VMEM((256, 256), jnp.bfloat16)],
        compiler_params=pltpu.CompilerParams(vmem_limit_bytes=48 * 2**20),
        name="final",
    )(core, own, other, vir_rows)


def coef_rows(ct, start, size):
    part = lax.dynamic_slice_in_dim(ct, start, size, 1)
    return jnp.concatenate([part[0:88], part[112:200], part[88:112]], axis=0)


def on_device(ao_slab, occ_coef, vir_coef, tile_index, pair_order):
    orb = lax.axis_index("orb")
    core = (orb % 2).astype(jnp.int32).reshape(1)
    n_pair = lax.axis_size("pair")
    n_orb = lax.axis_size("orb")
    owned = pair_order.shape[0] // n_pair
    other_core = [(o, o ^ 1) for o in range(n_orb)]

    slab = jnp.transpose(ao_slab, (1, 0, 2))
    ct = occ_coef.T
    ctp = coef_rows(ct, orb * slab.shape[0], slab.shape[0])
    keep, send = half_stage(core, slab, ct, ctp)
    recv = lax.ppermute(send, "orb", other_core)
    row, col = places_of(pair_order, n_pair)
    blocks = select_stage(row, col, keep, recv)
    groups = [[p * n_orb + z * 2 + c for p in range(n_pair) for z in range(n_orb // 2)] for c in range(2)]
    own = lax.all_to_all(blocks, ("pair", "orb"), 0, 0, axis_index_groups=groups, tiled=True)
    other = lax.ppermute(own, "orb", other_core)
    vir_rows = vir_coef[tile_index]
    return final_stage(core, own, other, vir_rows, owned)


def solution(mesh):
    return jax.shard_map(
        on_device,
        mesh=mesh,
        in_specs=(P("pair", "orb", None), P(), P(None, "orb"), P(), P()),
        out_specs=P("pair", None, "orb"),
        check_vma=False,
    )
```

```python
import jax
import jax.numpy as jnp
from jax import lax
from jax.experimental import pallas as pl
from jax.experimental.pallas import tpu as pltpu
from jax.sharding import PartitionSpec as P

NOCC = 200
COLS = 88
ROWS = 256
NPAIRS = NOCC * (NOCC + 1) // 2
KK = 8
HALF = 160
MSG = 10
CHUNK = 1280
LIMIT = 48 * 2**20


def fold(t):
    root = jnp.sqrt(8.0 * t.astype(jnp.float32) + 1.0)
    i = ((root - 1.0) * 0.5).astype(jnp.int32)
    i = jnp.where(i * (i + 1) > 2 * t, i - 1, i)
    i = jnp.where((i + 1) * (i + 2) <= 2 * t, i + 1, i)
    j = t - ((i * (i + 1)) >> 1)
    row = jnp.where(j < 88, i, jnp.where(j >= 113, j - 113, jnp.where(i >= 112, j + 112, j + 137)))
    col = jnp.where(j < 88, j, jnp.where((j >= 113) | (i >= 112), i - 112, i - 88))
    return row, jnp.where(t < NPAIRS, col, -1)


def half_kernel(orb_ref, ao_ref, ct_ref, keep_ref, send_ref, first_ref, ctp_ref):
    step = pl.program_id(0)
    block, kk, nq = ao_ref.shape
    np_ = ctp_ref.shape[1]
    for o in range(nq // np_):
        @pl.when((step == 0) & (orb_ref[0] == o))
        def _():
            ctp_ref[...] = ct_ref[:, o * np_:(o + 1) * np_]

    slab = ao_ref[...].reshape(block * kk, nq)
    first = lax.dot_general(slab, ct_ref[...], (((1,), (1,)), ((), ())), preferred_element_type=jnp.float32)
    at = pl.ds(pl.multiple_of(step * (block * kk), 8), block * kk)
    first_ref[0, at, :] = first[:, 0:128]
    first_ref[1, at, 0:NOCC - 128] = first[:, 128:NOCC]

    @pl.when(step == pl.num_programs(0) - 1)
    def _():
        lane = lax.broadcasted_iota(jnp.int32, (COLS, ROWS), 1)
        col = lax.broadcasted_iota(jnp.int32, (COLS, ROWS), 0)
        used = lax.broadcasted_iota(jnp.int32, (np_, 128), 1) < NOCC - 128
        ctp = ctp_ref[...]
        for k in range(kk):
            at = pl.ds(k, np_, stride=kk)
            right = jnp.where(used, first_ref[1, at, :], 0.0)
            fk = jnp.concatenate([first_ref[0, at, :], right], axis=1).astype(jnp.bfloat16)
            out = jnp.dot(ctp, fk, preferred_element_type=jnp.float32)
            o1 = out[0:88]
            o2 = out[112:200]
            o3 = jnp.concatenate([out[88:112], jnp.zeros((64, ROWS), jnp.float32)], axis=0)
            tri = jnp.where(lane >= col, o1, pltpu.roll(o2, ROWS - 113, 1))
            rest = jnp.where(lane < 225, pltpu.roll(o2, 112, 1), pltpu.roll(o3, 137, 1))
            keep_ref[k * COLS:(k + 1) * COLS, :] = jnp.where(lane < NOCC, tri, jnp.where(lane < 249, rest, 0.0))
        send_ref[...] = keep_ref[...].astype(jnp.bfloat16)


def half_stage(orb, slab, ct):
    np_, kk, nq = slab.shape
    block = 153
    kept = pl.BlockSpec((kk * COLS, ROWS), lambda i: (0, 0))
    return pl.pallas_call(
        half_kernel,
        grid=(np_ // block,),
        in_specs=[
            pl.BlockSpec(memory_space=pltpu.SMEM),
            pl.BlockSpec((block, kk, nq), lambda i: (i, 0, 0)),
            pl.BlockSpec((NOCC, nq), lambda i: (0, 0)),
        ],
        out_specs=[kept, kept],
        out_shape=[
            jax.ShapeDtypeStruct((kk * COLS, ROWS), jnp.float32),
            jax.ShapeDtypeStruct((kk * COLS, ROWS), jnp.bfloat16),
        ],
        scratch_shapes=[pltpu.VMEM((2, np_ * kk, 128), jnp.float32), pltpu.VMEM((NOCC, np_), jnp.bfloat16)],
        compiler_params=pltpu.CompilerParams(vmem_limit_bytes=LIMIT),
        name="half",
    )(orb, slab, ct)


def places_of(pair_order, core, n_pair):
    owned = pair_order.shape[0] // n_pair
    order = jnp.pad(pair_order.reshape(n_pair, owned), ((0, 0), (0, 2 * HALF - owned)), constant_values=NPAIRS)
    mine = jnp.where(core == 0, order[:, 0:HALF], order[:, HALF:2 * HALF])
    main = mine[:, 0:128].reshape(n_pair // 4, 512)
    left = mine[:, 128:HALF].reshape(n_pair // 4, 128)
    return jnp.concatenate([main, left], axis=1).reshape(-1, CHUNK)


def select_kernel(place_ref, keep_ref, recv_ref, vir_ref, out_ref, vbig_ref, tri_ref, row_ref, col_ref, stage_ref):
    line = lax.broadcasted_iota(jnp.int32, (256, 16), 0)
    s = lax.broadcasted_iota(jnp.int32, (256, 16), 1)
    hot = (s == ((line // 2) % 2) * 8 + line // 32).astype(jnp.bfloat16)
    vbig_ref[...] = jnp.dot(hot, vir_ref[...], preferred_element_type=jnp.float32).astype(jnp.bfloat16)
    tri_ref[...] = (keep_ref[...] + recv_ref[...].astype(jnp.float32)).astype(jnp.bfloat16)
    row, col = fold(place_ref[...])
    row_ref[...] = row
    col_ref[...] = col
    lane = lax.broadcasted_iota(jnp.int32, (KK, 128), 1)
    kpos = lax.broadcasted_iota(jnp.int32, (KK, 128), 0)
    first_col = lax.broadcasted_iota(jnp.int32, (8, CHUNK), 0)
    for ch in range(place_ref.shape[0]):
        row = row_ref[ch:ch + 1, :]
        col = col_ref[ch:ch + 1, :]
        hot = (lax.broadcasted_iota(jnp.int32, (ROWS, CHUNK), 0) == row).astype(jnp.bfloat16)
        picked = jnp.dot(tri_ref[...], hot, preferred_element_type=jnp.float32)
        accs = [jnp.zeros((8, CHUNK), jnp.float32)] * KK
        for v in range(COLS // 8):
            here = first_col + 8 * v == col
            accs = [jnp.where(here, picked[k * COLS + 8 * v:k * COLS + 8 * v + 8], a) for k, a in enumerate(accs)]
        vals = jnp.concatenate([jnp.sum(a, axis=0, keepdims=True) for a in accs], axis=0)
        for u in range(CHUNK // 640):
            left = vals[:, 640 * u + 512:640 * u + 640]
            turned = [left] + [pltpu.roll(left, 32 * s, 1) for s in (1, 2, 3)]
            for t in range(4):
                rest = turned[-t % 4]
                for j in (1, 2, 3):
                    rest = jnp.where(kpos // 2 == j, turned[(j - t) % 4], rest)
                rest = jnp.where(lane // 32 == kpos // 2, rest, 0.0)
                rest = rest[0:2] + rest[2:4] + rest[4:6] + rest[6:8]
                owner = 8 * ch + 4 * u + t
                for z in range(2):
                    at = (2 * owner + z) * MSG
                    stage_ref[at:at + 8, :] = vals[:, 640 * u + 128 * t:640 * u + 128 * (t + 1)]
                    stage_ref[at + 8:at + 10, :] = rest
    out_ref[...] = stage_ref[...].astype(jnp.bfloat16)


def select_stage(places, keep, recv, vir_rows):
    lines = places.shape[0] * (CHUNK // HALF) * 2 * MSG
    vmem = pl.BlockSpec(memory_space=pltpu.VMEM)
    return pl.pallas_call(
        select_kernel,
        out_shape=[
            jax.ShapeDtypeStruct((lines, 128), jnp.bfloat16),
            jax.ShapeDtypeStruct((256, 256), jnp.bfloat16),
        ],
        in_specs=[vmem] * 4,
        out_specs=[vmem, vmem],
        scratch_shapes=[
            pltpu.VMEM(keep.shape, jnp.bfloat16),
            pltpu.VMEM(places.shape, jnp.int32),
            pltpu.VMEM(places.shape, jnp.int32),
            pltpu.VMEM((lines, 128), jnp.float32),
        ],
        compiler_params=pltpu.CompilerParams(vmem_limit_bytes=LIMIT),
        name="select",
    )(places, keep, recv, vir_rows)


def final_kernel(share_ref, msg_ref, vbig_ref, *refs):
    out_ref, turned_ref, lines_ref = refs[-3:]
    step = pl.program_id(0)
    block = out_ref.shape[0]
    groups = turned_ref.shape[0]

    @pl.when(step == 0)
    def _():
        lines_ref[...] = msg_ref[...].astype(jnp.float32)
        for g in range(groups):
            at = 32 * MSG * g
            main = [lines_ref[pl.ds(at + k, 32, stride=MSG), :] for k in range(8)]
            turned_ref[g, 0:128, :] = jnp.concatenate(main, axis=0).T
            left = [lines_ref[pl.ds(at + k, 32, stride=MSG), :] for k in (8, 9)]
            left = jnp.concatenate(left, axis=0).T
            turned_ref[g, 128:HALF, :] = jnp.concatenate([left[32 * j:32 * (j + 1)] for j in range(4)], axis=1)

    lane = lax.broadcasted_iota(jnp.int32, (8, 256), 1)
    mask = (lane % 32) // 4 == lax.broadcasted_iota(jnp.int32, (8, 256), 0)
    at = pl.multiple_of(step * block, 8)
    for pair in range(groups // 2):
        parts = []
        for g in (2 * pair, 2 * pair + 1):
            rows = turned_ref[g, pl.ds(at, block), :]
            parts.append(jnp.where(mask[None], jnp.broadcast_to(rows[:, None, :], (block, 8, 256)), 0.0))
        lhs = jnp.concatenate(parts, axis=1).reshape(block * 16, 256).astype(jnp.bfloat16)
        res = jnp.dot(lhs, vbig_ref[...], preferred_element_type=jnp.float32)
        out_ref[:, 16 * pair:16 * (pair + 1), :] = res.reshape(block, 16, 256).astype(jnp.bfloat16)


def final_stage(share, msg, vbig, owned, into=None):
    block = 40
    steps = HALF // block
    held = [] if into is None else [into]
    return pl.pallas_call(
        final_kernel,
        grid_spec=pltpu.PrefetchScalarGridSpec(
            num_scalar_prefetch=1,
            grid=(steps,),
            in_specs=[
                pl.BlockSpec(msg.shape, lambda i, share: (0, 0)),
                pl.BlockSpec((256, 256), lambda i, share: (0, 0)),
            ] + [pl.BlockSpec(memory_space=pltpu.HBM)] * len(held),
            out_specs=pl.BlockSpec((block, 32, 256), lambda i, share: (share[0] * steps + i, 0, 0)),
            scratch_shapes=[
                pltpu.VMEM((4, HALF, 256), jnp.float32),
                pltpu.VMEM(msg.shape, jnp.float32),
            ],
        ),
        out_shape=jax.ShapeDtypeStruct((owned, 32, 256), jnp.bfloat16),
        input_output_aliases={3: 0} if held else {},
        compiler_params=pltpu.CompilerParams(vmem_limit_bytes=LIMIT),
        name="final",
    )(share, msg, vbig, *held)


def exchange(blocks, n_pair, n_orb):
    groups = [[p * n_orb + z * 2 + c for p in range(n_pair) for z in range(n_orb // 2)] for c in range(2)]
    packed = blocks.reshape(-1, MSG // 2, 2, 128)
    packed = lax.all_to_all(packed, ("pair", "orb"), 0, 0, axis_index_groups=groups, tiled=True)
    return packed.reshape(blocks.shape)


def on_device(ao_slab, occ_coef, vir_coef, tile_index, pair_order):
    n_pair = lax.axis_size("pair")
    n_orb = lax.axis_size("orb")
    orb = lax.axis_index("orb").astype(jnp.int32)
    core = orb & 1
    owned = pair_order.shape[0] // n_pair
    other_core = [(o, o ^ 1) for o in range(n_orb)]

    slab = jnp.transpose(ao_slab, (1, 0, 2))
    keep, send = half_stage(orb.reshape(1), slab, occ_coef.T)
    recv = lax.ppermute(send, "orb", other_core)
    places = places_of(pair_order, core, n_pair)
    blocks, vbig = select_stage(places, keep, recv, vir_coef[tile_index])
    own = exchange(blocks, n_pair, n_orb)
    other = lax.ppermute(own, "orb", other_core)
    mine = final_stage(core.reshape(1), own, vbig, owned)
    return final_stage((1 - core).reshape(1), other, vbig, owned, mine)


def solution(mesh):
    return jax.shard_map(
        on_device,
        mesh=mesh,
        in_specs=(P("pair", "orb", None), P(), P(None, "orb"), P(), P()),
        out_specs=P("pair", None, "orb"),
        check_vma=False,
    )
```

```python
import jax
import jax.numpy as jnp
from jax import lax
from jax.experimental import pallas as pl
from jax.experimental.pallas import tpu as pltpu
from jax.sharding import PartitionSpec as P

NOCC = 200
COLS = 88
ROWS = 256
NPAIRS = NOCC * (NOCC + 1) // 2
KK = 8
HALF = 160
MSG = 10
CHUNK = 1280
BLOCK = 40
LIMIT = 48 * 2**20


def fold(t):
    root = jnp.sqrt(8.0 * t.astype(jnp.float32) + 1.0)
    i = ((root - 1.0) * 0.5).astype(jnp.int32)
    i = jnp.where(i * (i + 1) > 2 * t, i - 1, i)
    i = jnp.where((i + 1) * (i + 2) <= 2 * t, i + 1, i)
    j = t - ((i * (i + 1)) >> 1)
    row = jnp.where(j < 88, i, jnp.where(j >= 113, j - 113, jnp.where(i >= 112, j + 112, j + 137)))
    col = jnp.where(j < 88, j, jnp.where((j >= 113) | (i >= 112), i - 112, i - 88))
    return row, jnp.where(t < NPAIRS, col, -1)


def half_kernel(orb_ref, ao_ref, ct_ref, keep_ref, send_ref, first_ref, ctp_ref):
    step = pl.program_id(0)
    block, kk, nq = ao_ref.shape
    np_ = ctp_ref.shape[1]
    for o in range(nq // np_):
        @pl.when((step == 0) & (orb_ref[0] == o))
        def _():
            ctp_ref[...] = ct_ref[:, o * np_:(o + 1) * np_]

    slab = ao_ref[...].reshape(block * kk, nq)
    first = lax.dot_general(slab, ct_ref[...], (((1,), (1,)), ((), ())), preferred_element_type=jnp.float32)
    at = pl.ds(pl.multiple_of(step * (block * kk), 8), block * kk)
    first_ref[0, at, :] = first[:, 0:128]
    first_ref[1, at, 0:NOCC - 128] = first[:, 128:NOCC]

    @pl.when(step == pl.num_programs(0) - 1)
    def _():
        lane = lax.broadcasted_iota(jnp.int32, (COLS, ROWS), 1)
        col = lax.broadcasted_iota(jnp.int32, (COLS, ROWS), 0)
        used = lax.broadcasted_iota(jnp.int32, (np_, 128), 1) < NOCC - 128
        ctp = ctp_ref[...]
        for k in range(kk):
            at = pl.ds(k, np_, stride=kk)
            right = jnp.where(used, first_ref[1, at, :], 0.0)
            fk = jnp.concatenate([first_ref[0, at, :], right], axis=1).astype(jnp.bfloat16)
            out = jnp.dot(ctp, fk, preferred_element_type=jnp.float32)
            o1 = out[0:88]
            o2 = out[112:200]
            o3 = jnp.concatenate([out[88:112], jnp.zeros((64, ROWS), jnp.float32)], axis=0)
            tri = jnp.where(lane >= col, o1, pltpu.roll(o2, ROWS - 113, 1))
            rest = jnp.where(lane < 225, pltpu.roll(o2, 112, 1), pltpu.roll(o3, 137, 1))
            keep_ref[k * COLS:(k + 1) * COLS, :] = jnp.where(lane < NOCC, tri, jnp.where(lane < 249, rest, 0.0))
        send_ref[...] = keep_ref[...].astype(jnp.bfloat16)


def half_stage(orb, slab, ct):
    np_, kk, nq = slab.shape
    block = 153
    kept = pl.BlockSpec((kk * COLS, ROWS), lambda i: (0, 0))
    return pl.pallas_call(
        half_kernel,
        grid=(np_ // block,),
        in_specs=[
            pl.BlockSpec(memory_space=pltpu.SMEM),
            pl.BlockSpec((block, kk, nq), lambda i: (i, 0, 0)),
            pl.BlockSpec((NOCC, nq), lambda i: (0, 0)),
        ],
        out_specs=[kept, kept],
        out_shape=[
            jax.ShapeDtypeStruct((kk * COLS, ROWS), jnp.float32),
            jax.ShapeDtypeStruct((kk * COLS, ROWS), jnp.bfloat16),
        ],
        scratch_shapes=[pltpu.VMEM((2, np_ * kk, 128), jnp.float32), pltpu.VMEM((NOCC, np_), jnp.bfloat16)],
        compiler_params=pltpu.CompilerParams(vmem_limit_bytes=LIMIT),
        name="half",
    )(orb, slab, ct)


def places_of(pair_order, core, n_pair):
    owned = pair_order.shape[0] // n_pair
    order = jnp.pad(pair_order.reshape(n_pair, owned), ((0, 0), (0, 2 * HALF - owned)), constant_values=NPAIRS)
    mine = jnp.where(core == 0, order[:, 0:HALF], order[:, HALF:2 * HALF])
    main = mine[:, 0:128].reshape(n_pair // 4, 512)
    left = mine[:, 128:HALF].reshape(n_pair // 4, 128)
    return jnp.concatenate([main, left], axis=1).reshape(-1, CHUNK)


def select_kernel(place_ref, keep_ref, recv_ref, vir_ref, out_ref, vbig_ref, tri_ref, row_ref, col_ref, stage_ref):
    line = lax.broadcasted_iota(jnp.int32, (256, 16), 0)
    s = lax.broadcasted_iota(jnp.int32, (256, 16), 1)
    hot = (s == ((line // 2) % 2) * 8 + line // 32).astype(jnp.bfloat16)
    vbig_ref[...] = jnp.dot(hot, vir_ref[...], preferred_element_type=jnp.float32).astype(jnp.bfloat16)
    tri_ref[...] = (keep_ref[...] + recv_ref[...].astype(jnp.float32)).astype(jnp.bfloat16)
    row, col = fold(place_ref[...])
    row_ref[...] = row
    col_ref[...] = col
    lane = lax.broadcasted_iota(jnp.int32, (KK, 128), 1)
    kpos = lax.broadcasted_iota(jnp.int32, (KK, 128), 0)
    first_col = lax.broadcasted_iota(jnp.int32, (8, CHUNK), 0)
    for ch in range(place_ref.shape[0]):
        row = row_ref[ch:ch + 1, :]
        col = col_ref[ch:ch + 1, :]
        hot = (lax.broadcasted_iota(jnp.int32, (ROWS, CHUNK), 0) == row).astype(jnp.bfloat16)
        picked = jnp.dot(tri_ref[...], hot, preferred_element_type=jnp.float32)
        accs = [jnp.zeros((8, CHUNK), jnp.float32)] * KK
        for v in range(COLS // 8):
            here = first_col + 8 * v == col
            accs = [jnp.where(here, picked[k * COLS + 8 * v:k * COLS + 8 * v + 8], a) for k, a in enumerate(accs)]
        vals = jnp.concatenate([jnp.sum(a, axis=0, keepdims=True) for a in accs], axis=0)
        for u in range(CHUNK // 640):
            left = vals[:, 640 * u + 512:640 * u + 640]
            turned = [left] + [pltpu.roll(left, 32 * s, 1) for s in (1, 2, 3)]
            for t in range(4):
                rest = turned[-t % 4]
                for j in (1, 2, 3):
                    rest = jnp.where(kpos // 2 == j, turned[(j - t) % 4], rest)
                rest = jnp.where(lane // 32 == kpos // 2, rest, 0.0)
                rest = rest[0:2] + rest[2:4] + rest[4:6] + rest[6:8]
                owner = 8 * ch + 4 * u + t
                for z in range(2):
                    at = (2 * owner + z) * MSG
                    stage_ref[at:at + 8, :] = vals[:, 640 * u + 128 * t:640 * u + 128 * (t + 1)]
                    stage_ref[at + 8:at + 10, :] = rest
    out_ref[...] = stage_ref[...].astype(jnp.bfloat16)


def select_stage(places, keep, recv, vir_rows):
    lines = places.shape[0] * (CHUNK // HALF) * 2 * MSG
    vmem = pl.BlockSpec(memory_space=pltpu.VMEM)
    return pl.pallas_call(
        select_kernel,
        out_shape=[
            jax.ShapeDtypeStruct((lines, 128), jnp.bfloat16),
            jax.ShapeDtypeStruct((256, 256), jnp.bfloat16),
        ],
        in_specs=[vmem] * 4,
        out_specs=[vmem, vmem],
        scratch_shapes=[
            pltpu.VMEM(keep.shape, jnp.bfloat16),
            pltpu.VMEM(places.shape, jnp.int32),
            pltpu.VMEM(places.shape, jnp.int32),
            pltpu.VMEM((lines, 128), jnp.float32),
        ],
        compiler_params=pltpu.CompilerParams(vmem_limit_bytes=LIMIT),
        name="select",
    )(places, keep, recv, vir_rows)


def final_kernel(share_ref, msg_ref, vbig_ref, *refs):
    out_ref, held_ref, turned_ref, lines_ref, sem = refs[-5:]
    groups = turned_ref.shape[0]
    share = share_ref[0]
    short = 2 * HALF - out_ref.shape[0]

    lines_ref[...] = msg_ref[...].astype(jnp.float32)
    for g in range(groups):
        at = 32 * MSG * g
        main = [lines_ref[pl.ds(at + k, 32, stride=MSG), :] for k in range(8)]
        turned_ref[g, 0:128, :] = jnp.concatenate(main, axis=0).T
        left = [lines_ref[pl.ds(at + k, 32, stride=MSG), :] for k in (8, 9)]
        left = jnp.concatenate(left, axis=0).T
        turned_ref[g, 128:HALF, :] = jnp.concatenate([left[32 * j:32 * (j + 1)] for j in range(4)], axis=1)

    lane = lax.broadcasted_iota(jnp.int32, (8, 256), 1)
    mask = (lane % 32) // 4 == lax.broadcasted_iota(jnp.int32, (8, 256), 0)

    def copy(at, rows):
        source = held_ref.at[pl.ds(at, rows)]
        return pltpu.make_async_copy(source, out_ref.at[pl.ds(share * HALF + at, rows)], sem.at[at // BLOCK])

    def each(act):
        for at in range(0, HALF, BLOCK):
            if at + BLOCK < HALF:
                act(at, BLOCK)

    def last(act):
        at = HALF - BLOCK

        @pl.when(share == 0)
        def _():
            act(at, BLOCK)

        @pl.when(share != 0)
        def _():
            act(at, BLOCK - short)

    for at in range(0, HALF, BLOCK):
        for pair in range(groups // 2):
            parts = []
            for g in (2 * pair, 2 * pair + 1):
                rows = turned_ref[g, at:at + BLOCK, :]
                parts.append(jnp.where(mask[None], jnp.broadcast_to(rows[:, None, :], (BLOCK, 8, 256)), 0.0))
            lhs = jnp.concatenate(parts, axis=1).reshape(BLOCK * 16, 256).astype(jnp.bfloat16)
            res = jnp.dot(lhs, vbig_ref[...], preferred_element_type=jnp.float32)
            res = res.reshape(BLOCK, 16, 256).astype(jnp.bfloat16)
            held_ref[at:at + BLOCK, 16 * pair:16 * (pair + 1), :] = res
        if at + BLOCK < HALF:
            copy(at, BLOCK).start()
    last(lambda at, rows: copy(at, rows).start())
    each(lambda at, rows: copy(at, rows).wait())
    last(lambda at, rows: copy(at, rows).wait())


def final_stage(share, msg, vbig, owned, into=None):
    held = [] if into is None else [into]
    vmem = pl.BlockSpec(memory_space=pltpu.VMEM)
    hbm = pl.BlockSpec(memory_space=pltpu.HBM)
    return pl.pallas_call(
        final_kernel,
        in_specs=[pl.BlockSpec(memory_space=pltpu.SMEM), vmem, vmem] + [hbm] * len(held),
        out_specs=hbm,
        out_shape=jax.ShapeDtypeStruct((owned, 32, 256), jnp.bfloat16),
        scratch_shapes=[
            pltpu.VMEM((HALF, 32, 256), jnp.bfloat16),
            pltpu.VMEM((4, HALF, 256), jnp.float32),
            pltpu.VMEM(msg.shape, jnp.float32),
            pltpu.SemaphoreType.DMA((HALF // BLOCK,)),
        ],
        input_output_aliases={3: 0} if held else {},
        compiler_params=pltpu.CompilerParams(vmem_limit_bytes=LIMIT),
        name="final",
    )(share, msg, vbig, *held)


def exchange(blocks, n_pair, n_orb):
    groups = [[p * n_orb + z * 2 + c for p in range(n_pair) for z in range(n_orb // 2)] for c in range(2)]
    packed = blocks.reshape(-1, MSG // 2, 2, 128)
    packed = lax.all_to_all(packed, ("pair", "orb"), 0, 0, axis_index_groups=groups, tiled=True)
    return packed.reshape(blocks.shape)


def on_device(ao_slab, occ_coef, vir_coef, tile_index, pair_order):
    n_pair = lax.axis_size("pair")
    n_orb = lax.axis_size("orb")
    orb = lax.axis_index("orb").astype(jnp.int32)
    core = orb & 1
    owned = pair_order.shape[0] // n_pair
    other_core = [(o, o ^ 1) for o in range(n_orb)]

    slab = jnp.transpose(ao_slab, (1, 0, 2))
    keep, send = half_stage(orb.reshape(1), slab, pltpu.with_memory_space_constraint(occ_coef.T, pltpu.HBM))
    recv = lax.ppermute(send, "orb", other_core)
    places = places_of(pair_order, core, n_pair)
    blocks, vbig = select_stage(places, keep, recv, vir_coef[tile_index])
    own = exchange(blocks, n_pair, n_orb)
    other = lax.ppermute(own, "orb", other_core)
    mine = final_stage(core.reshape(1), own, vbig, owned)
    return final_stage((1 - core).reshape(1), other, vbig, owned, mine)


def solution(mesh):
    return jax.shard_map(
        on_device,
        mesh=mesh,
        in_specs=(P("pair", "orb", None), P(), P(None, "orb"), P(), P()),
        out_specs=P("pair", None, "orb"),
        check_vma=False,
    )
```

```python
import jax
import jax.numpy as jnp
from jax import lax
from jax.experimental import pallas as pl
from jax.experimental.pallas import tpu as pltpu
from jax.sharding import PartitionSpec as P

NOCC = 200
COLS = 80
ROWS = 256
NPAIRS = NOCC * (NOCC + 1) // 2
KK = 8
HALF = 160
MSG = 10
CHUNK = 1280
BLOCK = 40
LIMIT = 48 * 2**20


def fold(t):
    root = jnp.sqrt(8.0 * t.astype(jnp.float32) + 1.0)
    i = ((root - 1.0) * 0.5).astype(jnp.int32)
    i = jnp.where(i * (i + 1) > 2 * t, i - 1, i)
    i = jnp.where((i + 1) * (i + 2) <= 2 * t, i + 1, i)
    j = t - ((i * (i + 1)) >> 1)
    low = i < 120
    row = jnp.where(j < 95, j + 161, jnp.where(j < 110, j + 146, j + 131))
    row = jnp.where(low, row, j + 120)
    row = jnp.where(j < 80, i, jnp.where(j > 120, j - 121, row))
    col = jnp.where(j < 95, i - 80, jnp.where(j < 110, i - 55, i - 45))
    col = jnp.where(j < 80, j, jnp.where(low, col, i - 120))
    return row, jnp.where(t < NPAIRS, col, -1)


def half_kernel(orb_ref, ao_ref, ct_ref, keep_ref, send_ref, first_ref, ctp_ref):
    step = pl.program_id(0)
    block, kk, nq = ao_ref.shape
    np_ = ctp_ref.shape[1]
    for o in range(nq // np_):
        @pl.when((step == 0) & (orb_ref[0] == o))
        def _():
            ctp_ref[...] = ct_ref[:, o * np_:(o + 1) * np_]

    slab = ao_ref[...].reshape(block * kk, nq)
    first = lax.dot_general(slab, ct_ref[...], (((1,), (1,)), ((), ())), preferred_element_type=jnp.float32)
    at = pl.ds(pl.multiple_of(step * (block * kk), 8), block * kk)
    first_ref[0, at, :] = first[:, 0:128]
    first_ref[1, at, 0:NOCC - 128] = first[:, 128:NOCC]

    @pl.when(step == pl.num_programs(0) - 1)
    def _():
        lane = lax.broadcasted_iota(jnp.int32, (COLS, 128), 1)
        col = lax.broadcasted_iota(jnp.int32, (COLS, 128), 0)
        ctp = ctp_ref[...]
        for k in range(kk):
            at = pl.ds(k, np_, stride=kk)
            fk = jnp.concatenate([first_ref[0, at, :], first_ref[1, at, :]], axis=1).astype(jnp.bfloat16)
            out = jnp.dot(ctp, fk, preferred_element_type=jnp.float32)
            a, b = out[:, 0:128], out[:, 128:256]
            wrap = jnp.where(lane < 7, pltpu.roll(a[120:200], 7, 1), pltpu.roll(b[120:200], 7, 1))
            mid = jnp.concatenate([a[80:120], a[95:120], a[110:120], jnp.zeros((5, 128), jnp.float32)], axis=0)
            low = jnp.where(col < 65, pltpu.roll(mid, 18, 1), pltpu.roll(mid, 3, 1))
            low = jnp.where(col < 40, pltpu.roll(mid, 33, 1), low)
            rest = jnp.where(lane < 113, pltpu.roll(a[120:200], 120, 1), low)
            rows = pl.ds(k * COLS, COLS)
            keep_ref[rows, 0:128] = jnp.where(lane >= col, a[0:80], wrap)
            keep_ref[rows, 128:256] = jnp.where(lane < 72, b[0:80], rest)
        send_ref[...] = keep_ref[...].astype(jnp.bfloat16)


def half_stage(orb, slab, ct):
    np_, kk, nq = slab.shape
    block = 153
    kept = pl.BlockSpec((kk * COLS, ROWS), lambda i: (0, 0))
    return pl.pallas_call(
        half_kernel,
        grid=(np_ // block,),
        in_specs=[
            pl.BlockSpec(memory_space=pltpu.SMEM),
            pl.BlockSpec((block, kk, nq), lambda i: (i, 0, 0)),
            pl.BlockSpec((NOCC, nq), lambda i: (0, 0)),
        ],
        out_specs=[kept, kept],
        out_shape=[
            jax.ShapeDtypeStruct((kk * COLS, ROWS), jnp.float32),
            jax.ShapeDtypeStruct((kk * COLS, ROWS), jnp.bfloat16),
        ],
        scratch_shapes=[pltpu.VMEM((2, np_ * kk, 128), jnp.float32), pltpu.VMEM((NOCC, np_), jnp.bfloat16)],
        compiler_params=pltpu.CompilerParams(vmem_limit_bytes=LIMIT),
        name="half",
    )(orb, slab, ct)


def places_of(pair_order, core, n_pair):
    owned = pair_order.shape[0] // n_pair
    order = jnp.pad(pair_order.reshape(n_pair, owned), ((0, 0), (0, 2 * HALF - owned)), constant_values=NPAIRS)
    mine = jnp.where(core == 0, order[:, 0:HALF], order[:, HALF:2 * HALF])
    main = mine[:, 0:128].reshape(n_pair // 4, 512)
    left = mine[:, 128:HALF].reshape(n_pair // 4, 128)
    return jnp.concatenate([main, left], axis=1).reshape(-1, CHUNK)


def select_kernel(place_ref, keep_ref, recv_ref, vir_ref, out_ref, vbig_ref, tri_ref, row_ref, col_ref, stage_ref):
    line = lax.broadcasted_iota(jnp.int32, (256, 16), 0)
    s = lax.broadcasted_iota(jnp.int32, (256, 16), 1)
    hot = (s == ((line // 2) % 2) * 8 + line // 32).astype(jnp.bfloat16)
    vbig_ref[...] = jnp.dot(hot, vir_ref[...], preferred_element_type=jnp.float32).astype(jnp.bfloat16)
    tri_ref[...] = (keep_ref[...] + recv_ref[...].astype(jnp.float32)).astype(jnp.bfloat16)
    row, col = fold(place_ref[...])
    row_ref[...] = row
    col_ref[...] = col
    lane = lax.broadcasted_iota(jnp.int32, (KK, 128), 1)
    kpos = lax.broadcasted_iota(jnp.int32, (KK, 128), 0)
    first_col = lax.broadcasted_iota(jnp.int32, (8, CHUNK), 0)
    for ch in range(place_ref.shape[0]):
        row = row_ref[ch:ch + 1, :]
        col = col_ref[ch:ch + 1, :]
        hot = (lax.broadcasted_iota(jnp.int32, (ROWS, CHUNK), 0) == row).astype(jnp.bfloat16)
        picked = jnp.dot(tri_ref[...], hot, preferred_element_type=jnp.float32)
        accs = [jnp.zeros((8, CHUNK), jnp.float32)] * KK
        for v in range(COLS // 8):
            here = first_col + 8 * v == col
            accs = [jnp.where(here, picked[k * COLS + 8 * v:k * COLS + 8 * v + 8], a) for k, a in enumerate(accs)]
        vals = jnp.concatenate([jnp.sum(a, axis=0, keepdims=True) for a in accs], axis=0)
        for u in range(CHUNK // 640):
            left = vals[:, 640 * u + 512:640 * u + 640]
            turned = [left] + [pltpu.roll(left, 32 * s, 1) for s in (1, 2, 3)]
            for t in range(4):
                rest = turned[-t % 4]
                for j in (1, 2, 3):
                    rest = jnp.where(kpos // 2 == j, turned[(j - t) % 4], rest)
                rest = jnp.where(lane // 32 == kpos // 2, rest, 0.0)
                rest = rest[0:2] + rest[2:4] + rest[4:6] + rest[6:8]
                owner = 8 * ch + 4 * u + t
                for z in range(2):
                    at = (2 * owner + z) * MSG
                    stage_ref[at:at + 8, :] = vals[:, 640 * u + 128 * t:640 * u + 128 * (t + 1)]
                    stage_ref[at + 8:at + 10, :] = rest
    out_ref[...] = stage_ref[...].astype(jnp.bfloat16)


def select_stage(places, keep, recv, vir_rows):
    lines = places.shape[0] * (CHUNK // HALF) * 2 * MSG
    vmem = pl.BlockSpec(memory_space=pltpu.VMEM)
    return pl.pallas_call(
        select_kernel,
        out_shape=[
            jax.ShapeDtypeStruct((lines, 128), jnp.bfloat16),
            jax.ShapeDtypeStruct((256, 256), jnp.bfloat16),
        ],
        in_specs=[vmem] * 4,
        out_specs=[vmem, vmem],
        scratch_shapes=[
            pltpu.VMEM(keep.shape, jnp.bfloat16),
            pltpu.VMEM(places.shape, jnp.int32),
            pltpu.VMEM(places.shape, jnp.int32),
            pltpu.VMEM((lines, 128), jnp.float32),
        ],
        compiler_params=pltpu.CompilerParams(vmem_limit_bytes=LIMIT),
        name="select",
    )(places, keep, recv, vir_rows)


def final_kernel(share_ref, msg_ref, vbig_ref, *refs):
    out_ref, held_ref, turned_ref, lines_ref, sem = refs[-5:]
    groups = turned_ref.shape[0]
    share = share_ref[0]
    short = 2 * HALF - out_ref.shape[0]

    lines_ref[...] = msg_ref[...].astype(jnp.float32)
    for g in range(groups):
        at = 32 * MSG * g
        main = [lines_ref[pl.ds(at + k, 32, stride=MSG), :] for k in range(8)]
        turned_ref[g, 0:128, :] = jnp.concatenate(main, axis=0).T
        left = [lines_ref[pl.ds(at + k, 32, stride=MSG), :] for k in (8, 9)]
        left = jnp.concatenate(left, axis=0).T
        turned_ref[g, 128:HALF, :] = jnp.concatenate([left[32 * j:32 * (j + 1)] for j in range(4)], axis=1)

    lane = lax.broadcasted_iota(jnp.int32, (8, 256), 1)
    mask = (lane % 32) // 4 == lax.broadcasted_iota(jnp.int32, (8, 256), 0)

    def copy(at, rows):
        source = held_ref.at[pl.ds(at, rows)]
        return pltpu.make_async_copy(source, out_ref.at[pl.ds(share * HALF + at, rows)], sem.at[at // BLOCK])

    def each(act):
        for at in range(0, HALF, BLOCK):
            if at + BLOCK < HALF:
                act(at, BLOCK)

    def last(act):
        at = HALF - BLOCK

        @pl.when(share == 0)
        def _():
            act(at, BLOCK)

        @pl.when(share != 0)
        def _():
            act(at, BLOCK - short)

    for at in range(0, HALF, BLOCK):
        for pair in range(groups // 2):
            parts = []
            for g in (2 * pair, 2 * pair + 1):
                rows = turned_ref[g, at:at + BLOCK, :]
                parts.append(jnp.where(mask[None], jnp.broadcast_to(rows[:, None, :], (BLOCK, 8, 256)), 0.0))
            lhs = jnp.concatenate(parts, axis=1).reshape(BLOCK * 16, 256).astype(jnp.bfloat16)
            res = jnp.dot(lhs, vbig_ref[...], preferred_element_type=jnp.float32)
            res = res.reshape(BLOCK, 16, 256).astype(jnp.bfloat16)
            held_ref[at:at + BLOCK, 16 * pair:16 * (pair + 1), :] = res
        if at + BLOCK < HALF:
            copy(at, BLOCK).start()
    last(lambda at, rows: copy(at, rows).start())
    each(lambda at, rows: copy(at, rows).wait())
    last(lambda at, rows: copy(at, rows).wait())


def final_stage(share, msg, vbig, owned, into=None):
    held = [] if into is None else [into]
    vmem = pl.BlockSpec(memory_space=pltpu.VMEM)
    hbm = pl.BlockSpec(memory_space=pltpu.HBM)
    return pl.pallas_call(
        final_kernel,
        in_specs=[pl.BlockSpec(memory_space=pltpu.SMEM), vmem, vmem] + [hbm] * len(held),
        out_specs=hbm,
        out_shape=jax.ShapeDtypeStruct((owned, 32, 256), jnp.bfloat16),
        scratch_shapes=[
            pltpu.VMEM((HALF, 32, 256), jnp.bfloat16),
            pltpu.VMEM((4, HALF, 256), jnp.float32),
            pltpu.VMEM(msg.shape, jnp.float32),
            pltpu.SemaphoreType.DMA((HALF // BLOCK,)),
        ],
        input_output_aliases={3: 0} if held else {},
        compiler_params=pltpu.CompilerParams(vmem_limit_bytes=LIMIT),
        name="final",
    )(share, msg, vbig, *held)


def exchange(blocks, n_pair, n_orb):
    groups = [[p * n_orb + z * 2 + c for p in range(n_pair) for z in range(n_orb // 2)] for c in range(2)]
    packed = blocks.reshape(-1, MSG // 2, 2, 128)
    packed = lax.all_to_all(packed, ("pair", "orb"), 0, 0, axis_index_groups=groups, tiled=True)
    return packed.reshape(blocks.shape)


def on_device(ao_slab, occ_coef, vir_coef, tile_index, pair_order):
    n_pair = lax.axis_size("pair")
    n_orb = lax.axis_size("orb")
    orb = lax.axis_index("orb").astype(jnp.int32)
    core = orb & 1
    owned = pair_order.shape[0] // n_pair
    other_core = [(o, o ^ 1) for o in range(n_orb)]

    slab = jnp.transpose(ao_slab, (1, 0, 2))
    keep, send = half_stage(orb.reshape(1), slab, pltpu.with_memory_space_constraint(occ_coef.T, pltpu.HBM))
    recv = lax.ppermute(send, "orb", other_core)
    places = places_of(pair_order, core, n_pair)
    blocks, vbig = select_stage(places, keep, recv, vir_coef[tile_index])
    own = exchange(blocks, n_pair, n_orb)
    other = lax.ppermute(own, "orb", other_core)
    mine = final_stage(core.reshape(1), own, vbig, owned)
    return final_stage((1 - core).reshape(1), other, vbig, owned, mine)


def solution(mesh):
    return jax.shard_map(
        on_device,
        mesh=mesh,
        in_specs=(P("pair", "orb", None), P(), P(None, "orb"), P(), P()),
        out_specs=P("pair", None, "orb"),
        check_vma=False,
    )
```

```python
import jax
import jax.numpy as jnp
from jax import lax
from jax.experimental import pallas as pl
from jax.experimental.pallas import tpu as pltpu
from jax.sharding import PartitionSpec as P

NOCC = 200
COLS = 80
ROWS = 256
NPAIRS = NOCC * (NOCC + 1) // 2
KK = 8
HALF = 160
MSG = 10
CHUNK = 2560
BLOCK = 40
EARLY = 80
LIMIT = 48 * 2**20


def fold(t):
    root = jnp.sqrt(8.0 * t.astype(jnp.float32) + 1.0)
    i = ((root - 1.0) * 0.5).astype(jnp.int32)
    i = jnp.where(i * (i + 1) > 2 * t, i - 1, i)
    i = jnp.where((i + 1) * (i + 2) <= 2 * t, i + 1, i)
    j = t - ((i * (i + 1)) >> 1)
    low = i < 120
    row = jnp.where(j < 95, j + 161, jnp.where(j < 110, j + 146, j + 131))
    row = jnp.where(low, row, j + 120)
    row = jnp.where(j < 80, i, jnp.where(j > 120, j - 121, row))
    col = jnp.where(j < 95, i - 80, jnp.where(j < 110, i - 55, i - 45))
    col = jnp.where(j < 80, j, jnp.where(low, col, i - 120))
    return row, jnp.where(t < NPAIRS, col, -1)


def half_kernel(orb_ref, ao_ref, ct_ref, keep_ref, send_ref, first_ref, ctp_ref):
    step = pl.program_id(0)
    block, kk, nq = ao_ref.shape
    np_ = ctp_ref.shape[1]
    for o in range(nq // np_):
        @pl.when((step == 0) & (orb_ref[0] == o))
        def _():
            ctp_ref[...] = ct_ref[:, o * np_:(o + 1) * np_]

    slab = ao_ref[...].reshape(block * kk, nq)
    first = lax.dot_general(slab, ct_ref[...], (((1,), (1,)), ((), ())), preferred_element_type=jnp.float32)
    at = pl.ds(pl.multiple_of(step * (block * kk), 8), block * kk)
    first_ref[0, at, :] = first[:, 0:128]
    first_ref[1, at, 0:NOCC - 128] = first[:, 128:NOCC]

    @pl.when(step == pl.num_programs(0) - 1)
    def _():
        lane = lax.broadcasted_iota(jnp.int32, (COLS, 128), 1)
        col = lax.broadcasted_iota(jnp.int32, (COLS, 128), 0)
        ctp = ctp_ref[...]
        for k in range(kk):
            at = pl.ds(k, np_, stride=kk)
            fk = jnp.concatenate([first_ref[0, at, :], first_ref[1, at, :]], axis=1).astype(jnp.bfloat16)
            out = jnp.dot(ctp, fk, preferred_element_type=jnp.float32)
            a, b = out[:, 0:128], out[:, 128:256]
            wrap = jnp.where(lane < 7, pltpu.roll(a[120:200], 7, 1), pltpu.roll(b[120:200], 7, 1))
            mid = jnp.concatenate([a[80:120], a[95:120], a[110:120], jnp.zeros((5, 128), jnp.float32)], axis=0)
            low = jnp.where(col < 65, pltpu.roll(mid, 18, 1), pltpu.roll(mid, 3, 1))
            low = jnp.where(col < 40, pltpu.roll(mid, 33, 1), low)
            rest = jnp.where(lane < 113, pltpu.roll(a[120:200], 120, 1), low)
            rows = pl.ds(k * COLS, COLS)
            keep_ref[rows, 0:128] = jnp.where(lane >= col, a[0:80], wrap)
            keep_ref[rows, 128:256] = jnp.where(lane < 72, b[0:80], rest)
        send_ref[...] = keep_ref[...].astype(jnp.bfloat16)


def half_stage(orb, slab, ct):
    np_, kk, nq = slab.shape
    block = 153
    kept = pl.BlockSpec((kk * COLS, ROWS), lambda i: (0, 0))
    return pl.pallas_call(
        half_kernel,
        grid=(np_ // block,),
        in_specs=[
            pl.BlockSpec(memory_space=pltpu.SMEM),
            pl.BlockSpec((block, kk, nq), lambda i: (i, 0, 0)),
            pl.BlockSpec((NOCC, nq), lambda i: (0, 0)),
        ],
        out_specs=[kept, kept],
        out_shape=[
            jax.ShapeDtypeStruct((kk * COLS, ROWS), jnp.float32),
            jax.ShapeDtypeStruct((kk * COLS, ROWS), jnp.bfloat16),
        ],
        scratch_shapes=[pltpu.VMEM((2, np_ * kk, 128), jnp.float32), pltpu.VMEM((NOCC, np_), jnp.bfloat16)],
        compiler_params=pltpu.CompilerParams(vmem_limit_bytes=LIMIT),
        name="half",
    )(orb, slab, ct)


def places_of(pair_order, core, n_pair):
    owned = pair_order.shape[0] // n_pair
    order = jnp.pad(pair_order.reshape(n_pair, owned), ((0, 0), (0, 2 * HALF - owned)), constant_values=NPAIRS)
    mine = jnp.where(core == 0, order[:, 0:HALF], order[:, HALF:2 * HALF])
    main = mine[:, 0:128].reshape(n_pair // 4, 512)
    left = mine[:, 128:HALF].reshape(n_pair // 4, 128)
    return jnp.concatenate([main, left], axis=1).reshape(-1, CHUNK)


def select_kernel(place_ref, keep_ref, recv_ref, vir_ref, out_ref, vbig_ref, tri_ref, row_ref, col_ref, stage_ref):
    line = lax.broadcasted_iota(jnp.int32, (256, 16), 0)
    s = lax.broadcasted_iota(jnp.int32, (256, 16), 1)
    hot = (s == ((line // 2) % 2) * 8 + line // 32).astype(jnp.bfloat16)
    vbig_ref[...] = jnp.dot(hot, vir_ref[...], preferred_element_type=jnp.float32).astype(jnp.bfloat16)
    tri_ref[...] = (keep_ref[...] + recv_ref[...].astype(jnp.float32)).astype(jnp.bfloat16)
    row, col = fold(place_ref[...])
    row_ref[...] = row
    col_ref[...] = col
    lane = lax.broadcasted_iota(jnp.int32, (KK, 128), 1)
    kpos = lax.broadcasted_iota(jnp.int32, (KK, 128), 0)
    first_col = lax.broadcasted_iota(jnp.int32, (8, CHUNK), 0)
    for ch in range(place_ref.shape[0]):
        row = row_ref[ch:ch + 1, :]
        col = col_ref[ch:ch + 1, :]
        same = lax.broadcasted_iota(jnp.int16, (ROWS, CHUNK), 0) == row.astype(jnp.int16)
        hot = jnp.where(same, jnp.ones((), jnp.bfloat16), jnp.zeros((), jnp.bfloat16))
        picked = jnp.dot(tri_ref[...], hot, preferred_element_type=jnp.float32)
        accs = [jnp.zeros((8, CHUNK), jnp.float32)] * KK
        for v in range(COLS // 8):
            here = first_col + 8 * v == col
            accs = [jnp.where(here, picked[k * COLS + 8 * v:k * COLS + 8 * v + 8], a) for k, a in enumerate(accs)]
        vals = jnp.concatenate([jnp.sum(a, axis=0, keepdims=True) for a in accs], axis=0)
        for u in range(CHUNK // 640):
            left = vals[:, 640 * u + 512:640 * u + 640]
            turned = [left] + [pltpu.roll(left, 32 * s, 1) for s in (1, 2, 3)]
            for t in range(4):
                rest = turned[-t % 4]
                for j in (1, 2, 3):
                    rest = jnp.where(kpos // 2 == j, turned[(j - t) % 4], rest)
                rest = jnp.where(lane // 32 == kpos // 2, rest, 0.0)
                rest = rest[0:2] + rest[2:4] + rest[4:6] + rest[6:8]
                owner = CHUNK // HALF * ch + 4 * u + t
                for z in range(2):
                    at = (2 * owner + z) * MSG
                    stage_ref[at:at + 8, :] = vals[:, 640 * u + 128 * t:640 * u + 128 * (t + 1)]
                    stage_ref[at + 8:at + 10, :] = rest
    out_ref[...] = stage_ref[...].astype(jnp.bfloat16)


def select_stage(places, keep, recv, vir_rows):
    lines = places.shape[0] * (CHUNK // HALF) * 2 * MSG
    vmem = pl.BlockSpec(memory_space=pltpu.VMEM)
    return pl.pallas_call(
        select_kernel,
        out_shape=[
            jax.ShapeDtypeStruct((lines, 128), jnp.bfloat16),
            jax.ShapeDtypeStruct((256, 256), jnp.bfloat16),
        ],
        in_specs=[vmem] * 4,
        out_specs=[vmem, vmem],
        scratch_shapes=[
            pltpu.VMEM(keep.shape, jnp.bfloat16),
            pltpu.VMEM(places.shape, jnp.int32),
            pltpu.VMEM(places.shape, jnp.int32),
            pltpu.VMEM((lines, 128), jnp.float32),
        ],
        compiler_params=pltpu.CompilerParams(vmem_limit_bytes=LIMIT),
        name="select",
    )(places, keep, recv, vir_rows)


def turn(msg_ref, lines_ref, turned_ref):
    lines_ref[...] = msg_ref[...].astype(jnp.float32)
    for g in range(turned_ref.shape[0]):
        at = 32 * MSG * g
        main = [lines_ref[pl.ds(at + k, 32, stride=MSG), :] for k in range(8)]
        turned_ref[g, 0:128, :] = jnp.concatenate(main, axis=0).T
        left = [lines_ref[pl.ds(at + k, 32, stride=MSG), :] for k in (8, 9)]
        left = jnp.concatenate(left, axis=0).T
        turned_ref[g, 128:HALF, :] = jnp.concatenate([left[32 * j:32 * (j + 1)] for j in range(4)], axis=1)


def quarter(turned_ref, vbig_ref, at, into_ref, to):
    lane = lax.broadcasted_iota(jnp.int32, (8, 256), 1)
    mask = (lane % 32) // 4 == lax.broadcasted_iota(jnp.int32, (8, 256), 0)
    for pair in range(turned_ref.shape[0] // 2):
        parts = []
        for g in (2 * pair, 2 * pair + 1):
            rows = turned_ref[g, at:at + BLOCK, :]
            parts.append(jnp.where(mask[None], jnp.broadcast_to(rows[:, None, :], (BLOCK, 8, 256)), 0.0))
        lhs = jnp.concatenate(parts, axis=1).reshape(BLOCK * 16, 256).astype(jnp.bfloat16)
        res = jnp.dot(lhs, vbig_ref[...], preferred_element_type=jnp.float32)
        res = res.reshape(BLOCK, 16, 256).astype(jnp.bfloat16)
        into_ref[to:to + BLOCK, 16 * pair:16 * (pair + 1), :] = res


def cut(share, act, source_ref, begin, rows, out_ref, at, sem):
    short = 2 * HALF - out_ref.shape[0]

    def copy(n):
        return pltpu.make_async_copy(source_ref.at[pl.ds(begin, n)], out_ref.at[pl.ds(share * HALF + at, n)], sem)

    @pl.when(share == 0)
    def _():
        act(copy(rows))

    @pl.when(share != 0)
    def _():
        act(copy(rows - short))


def own_kernel(share_ref, msg_ref, vbig_ref, out_ref, rest_ref, held_ref, turned_ref, lines_ref, sem):
    share = share_ref[0]

    def copy(at):
        source = held_ref.at[pl.ds(at, BLOCK)]
        return pltpu.make_async_copy(source, out_ref.at[pl.ds(share * HALF + at, BLOCK)], sem.at[at // BLOCK])

    turn(msg_ref, lines_ref, turned_ref)
    for at in range(0, EARLY, BLOCK):
        quarter(turned_ref, vbig_ref, at, held_ref, at)
        copy(at).start()
    for at in range(EARLY, HALF, BLOCK):
        quarter(turned_ref, vbig_ref, at, rest_ref, at - EARLY)
    for at in range(0, EARLY, BLOCK):
        copy(at).wait()


def other_kernel(share_ref, msg_ref, vbig_ref, rest_ref, into_ref, out_ref, held_ref, turned_ref, lines_ref, sem):
    del into_ref
    share = share_ref[0]
    end = HALF - BLOCK
    late = HALF // BLOCK

    def copy(at):
        source = held_ref.at[pl.ds(at, BLOCK)]
        return pltpu.make_async_copy(source, out_ref.at[pl.ds(share * HALF + at, BLOCK)], sem.at[at // BLOCK])

    cut(1 - share, lambda c: c.start(), rest_ref, 0, HALF - EARLY, out_ref, EARLY, sem.at[late])
    turn(msg_ref, lines_ref, turned_ref)
    for at in range(0, HALF, BLOCK):
        quarter(turned_ref, vbig_ref, at, held_ref, at)
        if at < end:
            copy(at).start()
    cut(share, lambda c: c.start(), held_ref, end, BLOCK, out_ref, end, sem.at[end // BLOCK])
    cut(1 - share, lambda c: c.wait(), rest_ref, 0, HALF - EARLY, out_ref, EARLY, sem.at[late])
    for at in range(0, end, BLOCK):
        copy(at).wait()
    cut(share, lambda c: c.wait(), held_ref, end, BLOCK, out_ref, end, sem.at[end // BLOCK])


def final_stage(core, own, other, vbig, owned):
    smem = pl.BlockSpec(memory_space=pltpu.SMEM)
    vmem = pl.BlockSpec(memory_space=pltpu.VMEM)
    hbm = pl.BlockSpec(memory_space=pltpu.HBM)
    whole = jax.ShapeDtypeStruct((owned, 32, 256), jnp.bfloat16)
    params = pltpu.CompilerParams(vmem_limit_bytes=LIMIT)

    def scratch(rows):
        return [
            pltpu.VMEM((rows, 32, 256), jnp.bfloat16),
            pltpu.VMEM((4, HALF, 256), jnp.float32),
            pltpu.VMEM(own.shape, jnp.float32),
            pltpu.SemaphoreType.DMA((HALF // BLOCK + 1,)),
        ]

    out, rest = pl.pallas_call(
        own_kernel,
        in_specs=[smem, vmem, vmem],
        out_specs=[hbm, vmem],
        out_shape=[whole, jax.ShapeDtypeStruct((HALF - EARLY, 32, 256), jnp.bfloat16)],
        scratch_shapes=scratch(EARLY),
        compiler_params=params,
        name="own",
    )(core.reshape(1), own, vbig)
    return pl.pallas_call(
        other_kernel,
        in_specs=[smem, vmem, vmem, vmem, hbm],
        out_specs=hbm,
        out_shape=whole,
        scratch_shapes=scratch(HALF),
        input_output_aliases={4: 0},
        compiler_params=params,
        name="other",
    )((1 - core).reshape(1), other, vbig, rest, out)


def exchange(blocks, n_pair, n_orb):
    groups = [[p * n_orb + z * 2 + c for p in range(n_pair) for z in range(n_orb // 2)] for c in range(2)]
    packed = blocks.reshape(-1, MSG // 2, 2, 128)
    packed = lax.all_to_all(packed, ("pair", "orb"), 0, 0, axis_index_groups=groups, tiled=True)
    return packed.reshape(blocks.shape)


def on_device(ao_slab, occ_coef, vir_coef, tile_index, pair_order):
    n_pair = lax.axis_size("pair")
    n_orb = lax.axis_size("orb")
    orb = lax.axis_index("orb").astype(jnp.int32)
    core = orb & 1
    owned = pair_order.shape[0] // n_pair
    other_core = [(o, o ^ 1) for o in range(n_orb)]

    slab = jnp.transpose(ao_slab, (1, 0, 2))
    keep, send = half_stage(orb.reshape(1), slab, pltpu.with_memory_space_constraint(occ_coef.T, pltpu.HBM))
    recv = lax.ppermute(send, "orb", other_core)
    places = places_of(pair_order, core, n_pair)
    blocks, vbig = select_stage(places, keep, recv, vir_coef[tile_index])
    own = exchange(blocks, n_pair, n_orb)
    other = lax.ppermute(own, "orb", other_core)
    return final_stage(core, own, other, vbig, owned)


def solution(mesh):
    return jax.shard_map(
        on_device,
        mesh=mesh,
        in_specs=(P("pair", "orb", None), P(), P(None, "orb"), P(), P()),
        out_specs=P("pair", None, "orb"),
        check_vma=False,
    )
```

```python
import jax
import jax.numpy as jnp
from jax import lax
from jax.experimental import pallas as pl
from jax.experimental.pallas import tpu as pltpu
from jax.sharding import PartitionSpec as P

NOCC = 200
COLS = 80
ROWS = 256
NPAIRS = NOCC * (NOCC + 1) // 2
KK = 8
HALF = 160
MSG = 10
CHUNK = 2560
BLOCK = 40
EARLY = 80
LIMIT = 48 * 2**20


def fold(t):
    root = jnp.sqrt(8.0 * t.astype(jnp.float32) + 1.0)
    i = ((root - 1.0) * 0.5).astype(jnp.int32)
    i = jnp.where(i * (i + 1) > 2 * t, i - 1, i)
    i = jnp.where((i + 1) * (i + 2) <= 2 * t, i + 1, i)
    j = t - ((i * (i + 1)) >> 1)
    low = i < 120
    row = jnp.where(j < 95, j + 161, jnp.where(j < 110, j + 146, j + 131))
    row = jnp.where(low, row, j + 120)
    row = jnp.where(j < 80, i, jnp.where(j > 120, j - 121, row))
    col = jnp.where(j < 95, i - 80, jnp.where(j < 110, i - 55, i - 45))
    col = jnp.where(j < 80, j, jnp.where(low, col, i - 120))
    return row, jnp.where(t < NPAIRS, col, -1)


def half_kernel(orb_ref, ao_ref, ct_ref, keep_ref, send_ref, first_ref, ctp_ref):
    step = pl.program_id(0)
    block, kk, nq = ao_ref.shape
    np_ = ctp_ref.shape[1]
    for o in range(nq // np_):
        @pl.when((step == 0) & (orb_ref[0] == o))
        def _():
            ctp_ref[...] = ct_ref[:, o * np_:(o + 1) * np_]

    slab = ao_ref[...].reshape(block * kk, nq)
    first = lax.dot_general(slab, ct_ref[...], (((1,), (1,)), ((), ())), preferred_element_type=jnp.float32)
    at = pl.ds(pl.multiple_of(step * (block * kk), 8), block * kk)
    first_ref[0, at, :] = first[:, 0:128]
    first_ref[1, at, 0:NOCC - 128] = first[:, 128:NOCC]

    @pl.when(step == pl.num_programs(0) - 1)
    def _():
        lane = lax.broadcasted_iota(jnp.int32, (COLS, 128), 1)
        col = lax.broadcasted_iota(jnp.int32, (COLS, 128), 0)
        ctp = ctp_ref[...]
        for k in range(kk):
            at = pl.ds(k, np_, stride=kk)
            fk = jnp.concatenate([first_ref[0, at, :], first_ref[1, at, :]], axis=1).astype(jnp.bfloat16)
            out = jnp.dot(ctp, fk, preferred_element_type=jnp.float32)
            a, b = out[:, 0:128], out[:, 128:256]
            wrap = jnp.where(lane < 7, pltpu.roll(a[120:200], 7, 1), pltpu.roll(b[120:200], 7, 1))
            mid = jnp.concatenate([a[80:120], a[95:120], a[110:120], jnp.zeros((5, 128), jnp.float32)], axis=0)
            low = jnp.where(col < 65, pltpu.roll(mid, 18, 1), pltpu.roll(mid, 3, 1))
            low = jnp.where(col < 40, pltpu.roll(mid, 33, 1), low)
            rest = jnp.where(lane < 113, pltpu.roll(a[120:200], 120, 1), low)
            rows = pl.ds(k * COLS, COLS)
            keep_ref[rows, 0:128] = jnp.where(lane >= col, a[0:80], wrap)
            keep_ref[rows, 128:256] = jnp.where(lane < 72, b[0:80], rest)
        send_ref[...] = keep_ref[...].astype(jnp.bfloat16)


def half_stage(orb, slab, ct):
    np_, kk, nq = slab.shape
    block = 153
    kept = pl.BlockSpec((kk * COLS, ROWS), lambda i: (0, 0))
    return pl.pallas_call(
        half_kernel,
        grid=(np_ // block,),
        in_specs=[
            pl.BlockSpec(memory_space=pltpu.SMEM),
            pl.BlockSpec((block, kk, nq), lambda i: (i, 0, 0)),
            pl.BlockSpec((NOCC, nq), lambda i: (0, 0)),
        ],
        out_specs=[kept, kept],
        out_shape=[
            jax.ShapeDtypeStruct((kk * COLS, ROWS), jnp.float32),
            jax.ShapeDtypeStruct((kk * COLS, ROWS), jnp.bfloat16),
        ],
        scratch_shapes=[pltpu.VMEM((2, np_ * kk, 128), jnp.float32), pltpu.VMEM((NOCC, np_), jnp.bfloat16)],
        compiler_params=pltpu.CompilerParams(vmem_limit_bytes=LIMIT),
        name="half",
    )(orb, slab, ct)


def places_of(pair_order, core, n_pair):
    owned = pair_order.shape[0] // n_pair
    order = jnp.pad(pair_order.reshape(n_pair, owned), ((0, 0), (0, 2 * HALF - owned)), constant_values=NPAIRS)
    mine = jnp.where(core == 0, order[:, 0:HALF], order[:, HALF:2 * HALF])
    main = mine[:, 0:128].reshape(n_pair // 4, 512)
    left = mine[:, 128:HALF].reshape(n_pair // 4, 128)
    return jnp.concatenate([main, left], axis=1).reshape(-1, CHUNK)


def select_kernel(place_ref, keep_ref, recv_ref, vir_ref, out_ref, vbig_ref, tri_ref, row_ref, col_ref, stage_ref):
    line = lax.broadcasted_iota(jnp.int32, (256, 16), 0)
    s = lax.broadcasted_iota(jnp.int32, (256, 16), 1)
    hot = (s == ((line // 2) % 2) * 8 + line // 32).astype(jnp.bfloat16)
    vbig_ref[...] = jnp.dot(hot, vir_ref[...], preferred_element_type=jnp.float32).astype(jnp.bfloat16)
    tri_ref[...] = (keep_ref[...] + recv_ref[...].astype(jnp.float32)).astype(jnp.bfloat16)
    row, col = fold(place_ref[...])
    row_ref[...] = row
    col_ref[...] = col
    lane = lax.broadcasted_iota(jnp.int32, (KK, 128), 1)
    kpos = lax.broadcasted_iota(jnp.int32, (KK, 128), 0)
    first_col = lax.broadcasted_iota(jnp.int16, (16, CHUNK), 0)
    for ch in range(place_ref.shape[0]):
        row = row_ref[ch:ch + 1, :]
        col = col_ref[ch:ch + 1, :]
        same = lax.broadcasted_iota(jnp.int16, (ROWS, CHUNK), 0) == row.astype(jnp.int16)
        hot = jnp.where(same, jnp.ones((), jnp.bfloat16), jnp.zeros((), jnp.bfloat16))
        picked = jnp.dot(tri_ref[...], hot, preferred_element_type=jnp.float32).astype(jnp.bfloat16)
        narrow = col.astype(jnp.int16)
        accs = [jnp.zeros((16, CHUNK), jnp.bfloat16)] * KK
        for v in range(COLS // 16):
            here = first_col + jnp.int16(16 * v) == narrow
            accs = [jnp.where(here, picked[k * COLS + 16 * v:k * COLS + 16 * v + 16], a) for k, a in enumerate(accs)]
        accs = [a.astype(jnp.float32) for a in accs]
        vals = jnp.concatenate([jnp.sum(a, axis=0, keepdims=True) for a in accs], axis=0)
        for u in range(CHUNK // 640):
            left = vals[:, 640 * u + 512:640 * u + 640]
            turned = [left] + [pltpu.roll(left, 32 * s, 1) for s in (1, 2, 3)]
            for t in range(4):
                rest = turned[-t % 4]
                for j in (1, 2, 3):
                    rest = jnp.where(kpos // 2 == j, turned[(j - t) % 4], rest)
                rest = jnp.where(lane // 32 == kpos // 2, rest, 0.0)
                rest = rest[0:2] + rest[2:4] + rest[4:6] + rest[6:8]
                owner = CHUNK // HALF * ch + 4 * u + t
                for z in range(2):
                    at = (2 * owner + z) * MSG
                    stage_ref[at:at + 8, :] = vals[:, 640 * u + 128 * t:640 * u + 128 * (t + 1)]
                    stage_ref[at + 8:at + 10, :] = rest
    out_ref[...] = stage_ref[...].astype(jnp.bfloat16)


def select_stage(places, keep, recv, vir_rows):
    lines = places.shape[0] * (CHUNK // HALF) * 2 * MSG
    vmem = pl.BlockSpec(memory_space=pltpu.VMEM)
    return pl.pallas_call(
        select_kernel,
        out_shape=[
            jax.ShapeDtypeStruct((lines, 128), jnp.bfloat16),
            jax.ShapeDtypeStruct((256, 256), jnp.bfloat16),
        ],
        in_specs=[vmem] * 4,
        out_specs=[vmem, vmem],
        scratch_shapes=[
            pltpu.VMEM(keep.shape, jnp.bfloat16),
            pltpu.VMEM(places.shape, jnp.int32),
            pltpu.VMEM(places.shape, jnp.int32),
            pltpu.VMEM((lines, 128), jnp.float32),
        ],
        compiler_params=pltpu.CompilerParams(vmem_limit_bytes=LIMIT),
        name="select",
    )(places, keep, recv, vir_rows)


def turn(msg_ref, lines_ref, turned_ref):
    lines_ref[...] = msg_ref[...].astype(jnp.float32)
    for g in range(turned_ref.shape[0]):
        at = 32 * MSG * g
        main = [lines_ref[pl.ds(at + k, 32, stride=MSG), :] for k in range(8)]
        turned_ref[g, 0:128, :] = jnp.concatenate(main, axis=0).T
        left = [lines_ref[pl.ds(at + k, 32, stride=MSG), :] for k in (8, 9)]
        left = jnp.concatenate(left, axis=0).T
        turned_ref[g, 128:HALF, :] = jnp.concatenate([left[32 * j:32 * (j + 1)] for j in range(4)], axis=1)


def quarter(turned_ref, vbig_ref, at, into_ref, to):
    lane = lax.broadcasted_iota(jnp.int32, (8, 256), 1)
    mask = (lane % 32) // 4 == lax.broadcasted_iota(jnp.int32, (8, 256), 0)
    for pair in range(turned_ref.shape[0] // 2):
        parts = []
        for g in (2 * pair, 2 * pair + 1):
            rows = turned_ref[g, at:at + BLOCK, :]
            parts.append(jnp.where(mask[None], jnp.broadcast_to(rows[:, None, :], (BLOCK, 8, 256)), 0.0))
        lhs = jnp.concatenate(parts, axis=1).reshape(BLOCK * 16, 256).astype(jnp.bfloat16)
        res = jnp.dot(lhs, vbig_ref[...], preferred_element_type=jnp.float32)
        res = res.reshape(BLOCK, 16, 256).astype(jnp.bfloat16)
        into_ref[to:to + BLOCK, 16 * pair:16 * (pair + 1), :] = res


def cut(share, act, source_ref, begin, rows, out_ref, at, sem):
    short = 2 * HALF - out_ref.shape[0]

    def copy(n):
        return pltpu.make_async_copy(source_ref.at[pl.ds(begin, n)], out_ref.at[pl.ds(share * HALF + at, n)], sem)

    @pl.when(share == 0)
    def _():
        act(copy(rows))

    @pl.when(share != 0)
    def _():
        act(copy(rows - short))


def own_kernel(share_ref, msg_ref, vbig_ref, out_ref, rest_ref, held_ref, turned_ref, lines_ref, sem):
    share = share_ref[0]

    def copy(at):
        source = held_ref.at[pl.ds(at, BLOCK)]
        return pltpu.make_async_copy(source, out_ref.at[pl.ds(share * HALF + at, BLOCK)], sem.at[at // BLOCK])

    turn(msg_ref, lines_ref, turned_ref)
    for at in range(0, EARLY, BLOCK):
        quarter(turned_ref, vbig_ref, at, held_ref, at)
        copy(at).start()
    for at in range(EARLY, HALF, BLOCK):
        quarter(turned_ref, vbig_ref, at, rest_ref, at - EARLY)
    for at in range(0, EARLY, BLOCK):
        copy(at).wait()


def other_kernel(share_ref, msg_ref, vbig_ref, rest_ref, into_ref, out_ref, held_ref, turned_ref, lines_ref, sem):
    del into_ref
    share = share_ref[0]
    end = HALF - BLOCK
    late = HALF // BLOCK

    def copy(at):
        source = held_ref.at[pl.ds(at, BLOCK)]
        return pltpu.make_async_copy(source, out_ref.at[pl.ds(share * HALF + at, BLOCK)], sem.at[at // BLOCK])

    cut(1 - share, lambda c: c.start(), rest_ref, 0, HALF - EARLY, out_ref, EARLY, sem.at[late])
    turn(msg_ref, lines_ref, turned_ref)
    for at in range(0, HALF, BLOCK):
        quarter(turned_ref, vbig_ref, at, held_ref, at)
        if at < end:
            copy(at).start()
    cut(share, lambda c: c.start(), held_ref, end, BLOCK, out_ref, end, sem.at[end // BLOCK])
    cut(1 - share, lambda c: c.wait(), rest_ref, 0, HALF - EARLY, out_ref, EARLY, sem.at[late])
    for at in range(0, end, BLOCK):
        copy(at).wait()
    cut(share, lambda c: c.wait(), held_ref, end, BLOCK, out_ref, end, sem.at[end // BLOCK])


def final_stage(core, own, other, vbig, owned):
    smem = pl.BlockSpec(memory_space=pltpu.SMEM)
    vmem = pl.BlockSpec(memory_space=pltpu.VMEM)
    hbm = pl.BlockSpec(memory_space=pltpu.HBM)
    whole = jax.ShapeDtypeStruct((owned, 32, 256), jnp.bfloat16)
    params = pltpu.CompilerParams(vmem_limit_bytes=LIMIT)

    def scratch(rows):
        return [
            pltpu.VMEM((rows, 32, 256), jnp.bfloat16),
            pltpu.VMEM((4, HALF, 256), jnp.float32),
            pltpu.VMEM(own.shape, jnp.float32),
            pltpu.SemaphoreType.DMA((HALF // BLOCK + 1,)),
        ]

    out, rest = pl.pallas_call(
        own_kernel,
        in_specs=[smem, vmem, vmem],
        out_specs=[hbm, vmem],
        out_shape=[whole, jax.ShapeDtypeStruct((HALF - EARLY, 32, 256), jnp.bfloat16)],
        scratch_shapes=scratch(EARLY),
        compiler_params=params,
        name="own",
    )(core.reshape(1), own, vbig)
    return pl.pallas_call(
        other_kernel,
        in_specs=[smem, vmem, vmem, vmem, hbm],
        out_specs=hbm,
        out_shape=whole,
        scratch_shapes=scratch(HALF),
        input_output_aliases={4: 0},
        compiler_params=params,
        name="other",
    )((1 - core).reshape(1), other, vbig, rest, out)


def exchange(blocks, n_pair, n_orb):
    groups = [[p * n_orb + z * 2 + c for p in range(n_pair) for z in range(n_orb // 2)] for c in range(2)]
    packed = blocks.reshape(-1, MSG // 2, 2, 128)
    packed = lax.all_to_all(packed, ("pair", "orb"), 0, 0, axis_index_groups=groups, tiled=True)
    return packed.reshape(blocks.shape)


def on_device(ao_slab, occ_coef, vir_coef, tile_index, pair_order):
    n_pair = lax.axis_size("pair")
    n_orb = lax.axis_size("orb")
    orb = lax.axis_index("orb").astype(jnp.int32)
    core = orb & 1
    owned = pair_order.shape[0] // n_pair
    other_core = [(o, o ^ 1) for o in range(n_orb)]

    slab = jnp.transpose(ao_slab, (1, 0, 2))
    keep, send = half_stage(orb.reshape(1), slab, pltpu.with_memory_space_constraint(occ_coef.T, pltpu.HBM))
    recv = lax.ppermute(send, "orb", other_core)
    places = places_of(pair_order, core, n_pair)
    blocks, vbig = select_stage(places, keep, recv, vir_coef[tile_index])
    own = exchange(blocks, n_pair, n_orb)
    other = lax.ppermute(own, "orb", other_core)
    return final_stage(core, own, other, vbig, owned)


def solution(mesh):
    return jax.shard_map(
        on_device,
        mesh=mesh,
        in_specs=(P("pair", "orb", None), P(), P(None, "orb"), P(), P()),
        out_specs=P("pair", None, "orb"),
        check_vma=False,
    )
```
